128 devices in a mesh: blk: 4 (over z_hi, core), group: 32 (over y, x, z_lo).
Axes of the slice: x: 4, y: 4, z: 4 (z_hi: 2, z_lo: 2; z = z_hi * 2 + z_lo), core: 2. Of those that a mesh axis runs over, the one named last changes fastest.
Arguments:
- image_embed: float32 [16384, 768], P(('blk', 'group')), may hold values from -0.25 to 0.25
- text_embed: float32 [16384, 768], P(('blk', 'group')), may hold values from -0.25 to 0.25
- log_temp: float32 [1], replicated, may hold values from 1.8 to 2.6
- bias: float32 [1], replicated, may hold values from -9 to -7
Outputs:
- image_grad: float32 [16384, 768], P(('blk', 'group'))
- text_grad: float32 [16384, 768], P(('blk', 'group'))
- scalars: float32 [3], replicated
The draws below stay inside these ranges and needn't reach their ends.
All inputs are finite; a program needn't handle non-finite values.
Results may differ from the reference program's by a relative error of at most 0.00045.
Values sent between devices are 32-bit elements; how exact they have to be, the bound alone decides.
No kernel may reach another device: no remote copies, remote signals or barrier semaphores. Data moves between devices by JAX's collectives and lax.ppermute only.
A program may use at most 128 MiB of HBM per device.

```python
import jax
import jax.numpy as jnp
from jax import lax

E = 768
PAIRS = 16384


def block_scale(own_key, dims, cuts, low, high):
    def one(position, parts):
        draws = jax.random.uniform(jax.random.fold_in(jax.random.fold_in(own_key, 6), position), (parts,), jnp.float32, low / len(cuts), high / len(cuts))
        return jnp.repeat(jnp.exp(draws), dims[position] // parts).reshape((-1,) + (1,) * (len(dims) - position - 1))

    factor_of = one(*cuts[0])
    for cut in cuts[1:]:
        factor_of = factor_of * one(*cut)
    return factor_of


def normal_values(stream_key, dims, scale, reach, split=(), kind=jnp.bfloat16):
    drawn = jax.random.normal(stream_key, dims, jnp.float32) * scale
    if len(split) > 0:
        drawn = block_scale(stream_key, dims, split, -0.22, 0.18) * drawn
    return jnp.clip(drawn, min=-reach, max=reach).astype(kind)


def setup_inputs(seed: int = 0) -> dict:
    arg_keys = jax.random.split(jax.random.key(seed), 5)
    image_embed = normal_values(arg_keys[0], (PAIRS, E), 0.036, 0.25, ((0, 128),), jnp.float32)
    text_embed = normal_values(arg_keys[1], (PAIRS, E), 0.036, 0.25, ((0, 128),), jnp.float32)
    log_temp = jnp.clip(jax.random.uniform(arg_keys[2], (1,), jnp.float32, 1.8, 2.6), 1.8, 2.6)
    bias = jnp.clip(jax.random.uniform(arg_keys[3], (1,), jnp.float32, -9.0, -7.0), -9.0, -7.0)
    return dict(image_embed=image_embed, text_embed=text_embed, log_temp=log_temp, bias=bias)


EPS = 1e-06

def unit_rows(embed):
    scale = lax.rsqrt(lax.optimization_barrier(jnp.sum(embed * embed, axis=1, keepdims=True)) + EPS)
    return (embed * scale, scale)

def reference(image_embed, text_embed, log_temp, bias):
    img_unit, img_scale = unit_rows(image_embed)
    txt_unit, txt_scale = unit_rows(text_embed)
    temp = jnp.exp(log_temp[0])
    shift = bias[0]
    total = image_embed.shape[0]
    width = image_embed.shape[1]
    block = total // 16
    img_blocks = img_unit.reshape(16, block, width)
    firsts = jnp.arange(16, dtype=jnp.int32) * block
    columns = jnp.arange(total, dtype=jnp.int32)

    def step(carry, inputs):
        txt_acc, sums = carry
        piece, first = inputs
        dots = jnp.dot(piece, txt_unit.T, precision=lax.Precision.HIGHEST, preferred_element_type=jnp.float32)
        logits = temp * dots + shift
        row_ids = first + jnp.arange(block, dtype=jnp.int32)
        sign = jnp.where(row_ids[:, None] == columns[None, :], 1.0, -1.0).astype(jnp.float32)
        loss_part = jnp.sum(jax.nn.softplus(-sign * logits))
        coef = -sign * jax.nn.sigmoid(-sign * logits)
        img_dir = temp * jnp.dot(coef, txt_unit, precision=lax.Precision.HIGHEST, preferred_element_type=jnp.float32)
        txt_acc = txt_acc + jnp.dot(coef.T, piece, precision=lax.Precision.HIGHEST, preferred_element_type=jnp.float32)
        sums = sums + jnp.stack([loss_part, jnp.sum(coef * (logits - shift)), jnp.sum(coef)])
        return ((txt_acc, sums), img_dir)
    start = (jnp.zeros((total, width), jnp.float32), jnp.zeros((3,), jnp.float32))
    (txt_acc, sums), img_dirs = lax.scan(step, start, (img_blocks, firsts))
    img_dir = img_dirs.reshape(total, width)
    txt_dir = temp * txt_acc
    image_grad = img_scale * (img_dir - img_unit * lax.optimization_barrier(jnp.sum(img_unit * img_dir, axis=1, keepdims=True)))
    text_grad = txt_scale * (txt_dir - txt_unit * lax.optimization_barrier(jnp.sum(txt_unit * txt_dir, axis=1, keepdims=True)))
    return (image_grad, text_grad, sums / total)
```

```python
import functools

import jax
import jax.numpy as jnp
import numpy as np
from jax import lax
from jax.experimental import pallas as pl
from jax.experimental.pallas import tpu as pltpu
from jax.sharding import Mesh, PartitionSpec as P

EPS = 1e-06
AXES = ("zh", "c", "y", "x", "zl")
SIZES = (2, 2, 4, 4, 2)
ROWS = 128
UNIT = 256
E = 768
CHUNKS = 8
CUTS = ((0, 88), (88, 176), (176, 256))
F32 = jnp.float32
BF16 = jnp.bfloat16


def pairs(move):
    out = []
    for here in range(128):
        zh, c, y, x, zl = (int(v) for v in np.unravel_index(here, SIZES))
        c, x, y, z = move(c, x, y, 2 * zh + zl)
        there = np.ravel_multi_index((z // 2, c, y, x, z % 2), SIZES)
        out.append((here, int(there)))
    return out


def image_mate(v):
    return v ^ 1


def text_mate(v):
    return (((v + 1) ^ 1) - 1) % 4


def across(dim):
    def move(c, x, y, z):
        at = [x, y, z]
        at[dim] = (image_mate if c == 0 else text_mate)(at[dim])
        return (c, *at)

    return pairs(move)


def other_core(a):
    return lax.ppermute(a, AXES, pairs(lambda c, x, y, z: (1 - c, x, y, z)))


def swap(dim, a):
    return lax.ppermute(a, AXES, across(dim))


def split(x):
    hi = x.astype(BF16)
    return hi, (x - hi.astype(F32)).astype(BF16)


def unit(x):
    return x * lax.rsqrt(jnp.sum(x * x, axis=1, keepdims=True) + EPS)


def mm(a, b, dims):
    return lax.dot_general(a, b, (dims, ((), ())), preferred_element_type=F32)


def mm3(a, b, dims):
    return mm(a[0], b[0], dims) + mm(a[0], b[1], dims) + mm(a[1], b[0], dims)


def fold(x):
    return jnp.sum(x.reshape(-1, 8, x.shape[-1]), axis=0)


SUB = 256


def block_kernel(par, core, *refs):
    d_refs, e_refs = refs[:CHUNKS], refs[CHUNKS : 2 * CHUNKS]
    keep, send, scal = refs[2 * CHUNKS : 2 * CHUNKS + 3]
    img, txt, ih, il, p_img, p_txt, zero, sums, in_sem, out_sem, z_sem, i_sem = refs[2 * CHUNKS + 3 :]
    c = core[0]
    temp, shift = par[0], par[1]

    @pl.when(c == 0)
    def _():
        for k in range(CHUNKS):
            pltpu.make_async_copy(d_refs[k].at[pl.ds(0, ROWS)], img.at[k], in_sem.at[0, k]).start()
        for k in range(CHUNKS):
            pltpu.make_async_copy(e_refs[k], txt.at[k], in_sem.at[1, k]).start()

    @pl.when(c == 1)
    def _():
        for k in range(CHUNKS):
            pltpu.make_async_copy(e_refs[k].at[pl.ds(ROWS, ROWS)], img.at[k], in_sem.at[0, k]).start()
        for k in range(CHUNKS):
            pltpu.make_async_copy(d_refs[k], txt.at[k], in_sem.at[1, k]).start()

    zero[...] = jnp.zeros_like(zero)
    p_img[...] = jnp.zeros_like(p_img)
    sums[...] = jnp.zeros_like(sums)
    for k in range(CHUNKS):
        pltpu.make_async_copy(d_refs[k].at[pl.ds(0, ROWS)], img.at[k], in_sem.at[0, k]).wait()
        hi, lo = split(unit(img[k]))
        ih[pl.ds(k * ROWS, ROWS)] = hi
        il[pl.ds(k * ROWS, ROWS)] = lo

    @pl.loop(0, CHUNKS)
    def _(k):
        pltpu.make_async_copy(d_refs[0], txt.at[k], in_sem.at[1, k]).wait()
        t = split(unit(txt[k]))
        total = None
        for s in range(CHUNKS * ROWS // SUB):
            rows = pl.ds(s * SUB, SUB)
            i = (ih[rows], il[rows])
            dots = mm3(i, t, ((1,), (1,)))
            logits = temp * dots + shift
            e = jnp.exp(logits)
            u = 1.0 + e
            r = 1.0 / u
            loss = jnp.log(u) + (e - (u - 1.0)) * r
            coef = e * r
            if s == 0:
                row = lax.broadcasted_iota(jnp.int32, (SUB, UNIT), 0)
                col = lax.broadcasted_iota(jnp.int32, (SUB, UNIT), 1)
                same = (row + c * ROWS == col) & (row < ROWS) & (k == 0)
                coef = jnp.where(same, -r, coef)
                loss = jnp.where(same, loss - logits, loss)
            sums[0] += fold(loss)
            sums[1] += fold(coef * dots)
            sums[2] += fold(coef)
            g = split(coef)
            p_img[rows] += mm3(g, t, ((1,), (0,)))
            part = mm3(g, i, ((0,), (0,)))
            total = part if total is None else total + part
        slot = k % 2

        @pl.when(k >= 2)
        def _():
            pltpu.make_async_copy(p_txt.at[slot], keep.at[0], out_sem.at[slot]).wait()

        p_txt[slot] = total * temp

        @pl.when(c == 0)
        def _():
            pltpu.make_async_copy(p_txt.at[slot], send.at[k], out_sem.at[slot]).start()

        @pl.when(c == 1)
        def _():
            pltpu.make_async_copy(p_txt.at[slot], keep.at[k], out_sem.at[slot]).start()

    p_img[...] = p_img[...] * temp

    for k in range(CHUNKS):
        mine = p_img.at[pl.ds(k * ROWS, ROWS)]

        @pl.when(c == 0)
        def _():
            pltpu.make_async_copy(mine, keep.at[k, pl.ds(0, ROWS)], i_sem.at[k]).start()
            pltpu.make_async_copy(zero, keep.at[k, pl.ds(ROWS, ROWS)], z_sem.at[k]).start()

        @pl.when(c == 1)
        def _():
            pltpu.make_async_copy(zero, send.at[k, pl.ds(0, ROWS)], z_sem.at[k]).start()
            pltpu.make_async_copy(mine, send.at[k, pl.ds(ROWS, ROWS)], i_sem.at[k]).start()

    scal[0] = sums[0]
    scal[1] = sums[1] * temp
    scal[2] = sums[2]
    for slot in range(2):
        pltpu.make_async_copy(p_txt.at[slot], keep.at[0], out_sem.at[slot]).wait()
    for k in range(CHUNKS):
        pltpu.make_async_copy(zero, keep.at[0, pl.ds(0, ROWS)], z_sem.at[k]).wait()
        pltpu.make_async_copy(zero, keep.at[0, pl.ds(0, ROWS)], i_sem.at[k]).wait()


def block(par, core, ds, es):
    hbm = pl.BlockSpec(memory_space=pl.ANY)
    smem = pl.BlockSpec(memory_space=pltpu.SMEM)
    wide = jax.ShapeDtypeStruct((CHUNKS, UNIT, E), F32)
    return pl.pallas_call(
        block_kernel,
        out_shape=(wide, wide, jax.ShapeDtypeStruct((3, 8, UNIT), F32)),
        in_specs=[smem, smem] + [hbm] * (2 * CHUNKS),
        out_specs=(hbm, hbm, pl.BlockSpec(memory_space=pltpu.VMEM)),
        scratch_shapes=[
            pltpu.VMEM((CHUNKS, ROWS, E), F32),
            pltpu.VMEM((CHUNKS, UNIT, E), F32),
            pltpu.VMEM((CHUNKS * ROWS, E), BF16),
            pltpu.VMEM((CHUNKS * ROWS, E), BF16),
            pltpu.VMEM((CHUNKS * ROWS, E), F32),
            pltpu.VMEM((2, UNIT, E), F32),
            pltpu.VMEM((ROWS, E), F32),
            pltpu.VMEM((3, 8, UNIT), F32),
            pltpu.SemaphoreType.DMA((2, CHUNKS)),
            pltpu.SemaphoreType.DMA((2,)),
            pltpu.SemaphoreType.DMA((CHUNKS,)),
            pltpu.SemaphoreType.DMA((CHUNKS,)),
        ],
        compiler_params=pltpu.CompilerParams(vmem_limit_bytes=48 * 1024 * 1024),
        cost_estimate=pl.CostEstimate(
            flops=18 * CHUNKS * ROWS * CHUNKS * UNIT * E,
            bytes_accessed=4 * 40 * UNIT * E,
            transcendentals=3 * CHUNKS * ROWS * CHUNKS * UNIT,
        ),
        name="pair_block",
    )(par, core, *ds, *es)


def gather(own):
    dx, dy, dz = swap(0, own), swap(1, own), swap(2, own)
    dxy, dyz, dzx = swap(1, dx), swap(2, dy), swap(0, dz)
    far = [swap(d, a[lo:hi]) for d, a, (lo, hi) in zip((2, 0, 1), (dxy, dyz, dzx), CUTS)]
    return [own, dx, dy, dz, dxy, dyz, dzx, jnp.concatenate(far)]


def scatter(q):
    own, dx, dy, dz, dxy, dyz, dzx, far = q
    two = []
    for d, a, (lo, hi) in zip((2, 0, 1), (dxy, dyz, dzx), CUTS):
        two.append(a.at[lo:hi].add(swap(d, far[lo:hi])))
    one = [a + swap(d, b) for d, a, b in zip((1, 2, 0), (dx, dy, dz), two)]
    for d, a in zip((0, 1, 2), one):
        own = own + swap(d, a)
    return own


def back(embed, direction):
    scale = lax.rsqrt(jnp.sum(embed * embed, axis=1, keepdims=True) + EPS)
    u = embed * scale
    return scale * (direction - u * jnp.sum(u * direction, axis=1, keepdims=True))


def body(image_embed, text_embed, log_temp, bias):
    c = lax.axis_index("c")
    total = image_embed.shape[0] * 128
    par = jnp.concatenate([jnp.exp(log_temp), bias])
    mine = jnp.where(c == 0, image_embed, text_embed)
    rec = other_core(jnp.where(c == 0, text_embed, image_embed))
    own = jnp.concatenate([jnp.where(c == 0, mine, rec), jnp.where(c == 0, rec, mine)])
    ds = gather(own)
    es = [other_core(d) for d in ds]
    keep, send, scal = block(par, c.astype(jnp.int32).reshape(1), ds, es)
    got = other_core(send)
    q = [keep[k] + got[k] for k in range(CHUNKS)]
    sums = lax.psum(jnp.sum(scal, axis=(1, 2)), AXES)
    acc = scatter(q)
    low, high = acc[:ROWS], acc[ROWS:]
    rec = other_core(jnp.where(c == 0, high, low))
    img_dir = jnp.where(c == 0, low, rec)
    txt_dir = jnp.where(c == 0, rec, high)
    return back(image_embed, img_dir), back(text_embed, txt_dir), sums / total


def solution(mesh):
    fine = Mesh(mesh.devices.reshape(SIZES), AXES)
    wide = P(AXES, None)
    return jax.shard_map(
        body, mesh=fine, in_specs=(wide, wide, P(), P()), out_specs=(wide, wide, P()), check_vma=False
    )
```

```python
import functools

import jax
import jax.numpy as jnp
import numpy as np
from jax import lax
from jax.experimental import pallas as pl
from jax.experimental.pallas import tpu as pltpu
from jax.sharding import Mesh, PartitionSpec as P

EPS = 1e-06
AXES = ("zh", "c", "y", "x", "zl")
SIZES = (2, 2, 4, 4, 2)
ROWS = 128
UNIT = 256
E = 768
CHUNKS = 8
NEAR = 4
HALF = NEAR * ROWS
SUB = 256
MIB = 1024 * 1024
F32 = jnp.float32
BF16 = jnp.bfloat16


def pairs(move):
    out = []
    for here in range(128):
        zh, c, y, x, zl = (int(v) for v in np.unravel_index(here, SIZES))
        c, x, y, z = move(c, x, y, 2 * zh + zl)
        there = np.ravel_multi_index((z // 2, c, y, x, z % 2), SIZES)
        out.append((here, int(there)))
    return out


def image_mate(v):
    return v ^ 1


def text_mate(v):
    return (((v + 1) ^ 1) - 1) % 4


def across(dim):
    def move(c, x, y, z):
        at = [x, y, z]
        at[dim] = (image_mate if c == 0 else text_mate)(at[dim])
        return (c, *at)

    return pairs(move)


def other_core(a):
    return lax.ppermute(a, AXES, pairs(lambda c, x, y, z: (1 - c, x, y, z)))


def swap(dim, a):
    return lax.ppermute(a, AXES, across(dim))


def split(x):
    hi = x.astype(BF16)
    return hi, (x - hi.astype(F32)).astype(BF16)


def unit(x):
    return x * lax.rsqrt(jnp.sum(x * x, axis=1, keepdims=True) + EPS)


def mm(a, b, dims):
    return lax.dot_general(a, b, (dims, ((), ())), preferred_element_type=F32)


def mm3(a, b, dims):
    return mm(a[0], b[0], dims) + mm(a[0], b[1], dims) + mm(a[1], b[0], dims)


def fold(x):
    return jnp.sum(x.reshape(-1, 8, x.shape[-1]), axis=0)


def prep_images(c, d_refs, e_refs, hi_ref, lo_ref):
    for k in range(NEAR):
        hi, lo = split(unit(jnp.where(c == 0, d_refs[k][:ROWS], e_refs[k][ROWS:])))
        hi_ref[pl.ds(k * ROWS, ROWS)] = hi
        lo_ref[pl.ds(k * ROWS, ROWS)] = lo


def prep_text(c, d_ref, e_ref, hi_ref, lo_ref, k):
    hi, lo = split(unit(jnp.where(c == 0, e_ref[...], d_ref[...])))
    hi_ref[k] = hi
    lo_ref[k] = lo


def work(par, ts, tasks, same, sums, totals):
    def image(j):
        rows = pl.ds(tasks[j][4], SUB)
        return tasks[j][1][rows], tasks[j][2][rows]

    n = len(tasks)
    totals = list(totals)
    ahead = mm3(image(0), ts[tasks[0][0]], ((1,), (1,)))
    coefs = None
    for j in range(n + 1):
        dots = ahead
        if j + 1 < n:
            ahead = mm3(image(j + 1), ts[tasks[j + 1][0]], ((1,), (1,)))
        if coefs is not None:
            at, _, _, partial, first = tasks[j - 1]
            partial[pl.ds(first, SUB)] += mm3(coefs, ts[at], ((1,), (0,)))
            part = mm3(coefs, image(j - 1), ((0,), (0,)))
            totals[at] = part if totals[at] is None else totals[at] + part
        if j < n:
            logits = par[0] * dots + par[1]
            e = jnp.exp(logits)
            u = 1.0 + e
            r = 1.0 / u
            loss = jnp.log(u) + (e - (u - 1.0)) * r
            coef = e * r
            if same is not None and j == 0:
                coef = jnp.where(same, -r, coef)
                loss = jnp.where(same, loss - logits, loss)
            sums[0] += fold(loss)
            sums[1] += fold(coef * dots)
            sums[2] += fold(coef)
            coefs = split(coef)
    return totals


def total_kernel(core, *refs):
    parts, mine, theirs = refs[:-2], refs[-2], refs[-1]

    def put(a, b):
        for half, dest in ((a, mine), (b, theirs)):
            rows = pl.ds(half * ROWS, ROWS)
            dest[...] = (parts[0][rows] + parts[1][rows]) + (parts[2][rows] + parts[3][rows]) + parts[4][rows]

    @pl.when(core[0] == 0)
    def _():
        put(0, 1)

    @pl.when(core[0] == 1)
    def _():
        put(1, 0)


def grad_of(embed, direction, out):
    scale = lax.rsqrt(jnp.sum(embed * embed, axis=1, keepdims=True) + EPS)
    u = embed * scale
    out[...] = scale * (direction - u * jnp.sum(u * direction, axis=1, keepdims=True))


def grad_kernel(par, core, image, text, mine, theirs, d_image, d_text):
    @pl.when(core[0] == 0)
    def _():
        grad_of(image[...], par[0] * mine[...], d_image)
        grad_of(text[...], par[0] * theirs[...], d_text)

    @pl.when(core[0] == 1)
    def _():
        grad_of(image[...], par[0] * theirs[...], d_image)
        grad_of(text[...], par[0] * mine[...], d_text)


def near_kernel(par, core, *refs):
    d_refs, e_refs = refs[:NEAR], refs[NEAR : 2 * NEAR]
    p_txt, p_img, ih, il, th, tl, sums = refs[2 * NEAR :]
    c = core[0]
    p_img[...] = jnp.zeros_like(p_img)
    sums[...] = jnp.zeros_like(sums)
    prep_images(c, d_refs, e_refs, ih, il)
    for k in range(NEAR):
        prep_text(c, d_refs[k], e_refs[k], th, tl, k)
    row = lax.broadcasted_iota(jnp.int32, (SUB, UNIT), 0)
    col = lax.broadcasted_iota(jnp.int32, (SUB, UNIT), 1)

    @pl.loop(0, NEAR // 2)
    def _(i):
        same = (row + c * ROWS == col) & (row < ROWS) & (i == 0)
        ts = [(th[2 * i + h], tl[2 * i + h]) for h in range(2)]
        tasks = [(h, ih, il, p_img, m * SUB) for h in range(2) for m in range(HALF // SUB)]
        out = work(par, ts, tasks, same, sums, [None, None])
        for h in range(2):
            p_txt[2 * i + h] = out[h]


def rest_kernel(par, core, *refs):
    d_refs, e_refs = refs[:NEAR], refs[NEAR : 2 * NEAR]
    p_txt, p_img, ihn, iln, thn, tln, i_sums = refs[2 * NEAR : 2 * NEAR + 7]
    outs = refs[2 * NEAR + 7 :]
    keep_far, send_far = outs[:NEAR], outs[NEAR : 2 * NEAR]
    keep_near, send_near, line, ihf, ilf, thf, tlf, pin, pif, sums = outs[2 * NEAR :]
    c = core[0]
    pin[...] = p_img[...]
    pif[...] = jnp.zeros_like(pif)
    sums[...] = i_sums[...]
    prep_images(c, d_refs, e_refs, ihf, ilf)
    for k in range(NEAR):
        prep_text(c, d_refs[k], e_refs[k], thf, tlf, k)

    def put(keep, send, total):
        @pl.when(c == 0)
        def _():
            send[...] = total

        @pl.when(c == 1)
        def _():
            keep[...] = total

    @pl.loop(0, NEAR // 2)
    def _(i):
        ts = [(thn[2 * i + h], tln[2 * i + h]) for h in range(2)]
        tasks = [(h, ihf, ilf, pif, m * SUB) for h in range(2) for m in range(HALF // SUB)]
        out = work(par, ts, tasks, None, sums, [p_txt[2 * i], p_txt[2 * i + 1]])
        for h in range(2):
            put(keep_near.at[2 * i + h], send_near.at[2 * i + h], out[h])

    @pl.loop(0, NEAR)
    def _(k):
        tasks = [(0, ihn, iln, pin, m * SUB) for m in range(HALF // SUB)]
        tasks += [(0, ihf, ilf, pif, m * SUB) for m in range(HALF // SUB)]
        total = work(par, [(thf[k], tlf[k])], tasks, None, sums, [None])[0]
        for j in range(NEAR):

            @pl.when(k == j)
            def _():
                put(keep_far[j], send_far[j], total)

    lane = lax.broadcasted_iota(jnp.int32, line.shape, 1)
    values = jnp.zeros(line.shape, F32)
    for j, factor in enumerate((1.0, par[0], 1.0)):
        values = jnp.where(lane == j, jnp.sum(sums[j]) * factor, values)
    line[...] = values
    blank = jnp.zeros((ROWS, E), F32)

    @pl.when(c == 0)
    def _():
        for k in range(NEAR):
            for src, dest in ((pin, keep_near.at[k]), (pif, keep_far[k])):
                dest[:ROWS] = src[pl.ds(k * ROWS, ROWS)]
                dest[ROWS:] = blank

    @pl.when(c == 1)
    def _():
        for k in range(NEAR):
            for src, dest in ((pin, send_near.at[k]), (pif, send_far[k])):
                dest[:ROWS] = blank
                dest[ROWS:] = src[pl.ds(k * ROWS, ROWS)]


SMEM = pl.BlockSpec(memory_space=pltpu.SMEM)
VMEM = pl.BlockSpec(memory_space=pltpu.VMEM)
SUMS = jax.ShapeDtypeStruct((3, 8, UNIT), F32)
CHUNK = jax.ShapeDtypeStruct((UNIT, E), F32)
FOUR = jax.ShapeDtypeStruct((NEAR, UNIT, E), F32)


def cost(pairs_done):
    return pl.CostEstimate(flops=0 * pairs_done, bytes_accessed=4 * UNIT * E, transcendentals=0)


def near_block(par, core, ds, es):
    image = jax.ShapeDtypeStruct((HALF, E), BF16)
    text = jax.ShapeDtypeStruct((NEAR, UNIT, E), BF16)
    return pl.pallas_call(
        near_kernel,
        out_shape=(FOUR, jax.ShapeDtypeStruct((HALF, E), F32), image, image, text, text, SUMS),
        in_specs=[SMEM, SMEM] + [VMEM] * (2 * NEAR),
        out_specs=(VMEM,) * 7,
        compiler_params=pltpu.CompilerParams(vmem_limit_bytes=16 * MIB),
        cost_estimate=cost(NEAR * NEAR * ROWS * UNIT),
        name="near_block",
    )(par, core, *ds, *es)


def rest_block(par, core, ds, es, before):
    image = pltpu.VMEM((HALF, E), BF16)
    text = pltpu.VMEM((NEAR, UNIT, E), BF16)
    return pl.pallas_call(
        rest_kernel,
        out_shape=(CHUNK,) * (2 * NEAR) + (FOUR, FOUR, jax.ShapeDtypeStruct((128, 128), F32)),
        in_specs=[SMEM, SMEM] + [VMEM] * (2 * NEAR + 7),
        out_specs=(VMEM,) * (2 * NEAR + 3),
        scratch_shapes=[image, image, text, text, pltpu.VMEM((HALF, E), F32), pltpu.VMEM((HALF, E), F32), pltpu.VMEM((3, 8, UNIT), F32)],
        compiler_params=pltpu.CompilerParams(vmem_limit_bytes=24 * MIB),
        cost_estimate=cost((CHUNKS * CHUNKS - NEAR * NEAR) * ROWS * UNIT),
        name="rest_block",
    )(par, core, *ds, *es, *before)


def small(kernel, scalars, arrays, rows, name):
    shape = jax.ShapeDtypeStruct((rows, E), F32)
    return pl.pallas_call(
        kernel,
        out_shape=(shape, shape),
        in_specs=[SMEM] * len(scalars) + [VMEM] * len(arrays),
        out_specs=(VMEM, VMEM),
        compiler_params=pltpu.CompilerParams(vmem_limit_bytes=8 * MIB),
        cost_estimate=cost(0),
        name=name,
    )(*scalars, *arrays)


def corner(a):
    def move(c, x, y, z):
        mate = image_mate if c == 0 else text_mate
        return (c, mate(x), mate(y), mate(z))

    return lax.ppermute(a, AXES, pairs(move))


def after(a, *others):
    return lax.optimization_barrier((a, *others))[0]


def all_sum(line):
    return jnp.sum(lax.all_to_all(line, AXES, 0, 0, tiled=True), axis=0)


def body(image_embed, text_embed, log_temp, bias):
    c = lax.axis_index("c")
    total = image_embed.shape[0] * 128
    temp = jnp.exp(log_temp)
    par = jnp.concatenate([temp, bias])
    core = c.astype(jnp.int32).reshape(1)
    img_rec, txt_rec = other_core(image_embed), other_core(text_embed)
    first = c == 0
    own = jnp.concatenate([jnp.where(first, image_embed, txt_rec), jnp.where(first, img_rec, text_embed)])
    e_own = jnp.concatenate([jnp.where(first, text_embed, img_rec), jnp.where(first, txt_rec, image_embed)])
    one = [swap(d, own) for d in range(3)]
    last = corner(after(own, *one))
    zx = swap(0, one[2])
    yz = swap(2, one[1])
    xy = swap(1, one[0])
    near, e_near = [own] + one, [e_own] + [other_core(after(a, *one)) for a in one]
    before = near_block(par, core, near, e_near)
    rest = [xy, yz, zx, last]
    e_rest = [other_core(after(a, before[-1], *rest)) for a in rest]
    outs = rest_block(par, core, rest, e_rest, before)
    keep, send, (keep_near, send_near, line) = outs[:NEAR], outs[NEAR : 2 * NEAR], outs[2 * NEAR :]
    q = [k + other_core(s) for k, s in zip(keep, send)]
    got = other_core(after(send_near, *q[:3]))
    q_near = [keep_near[k] + got[k] for k in range(NEAR)]
    two = [swap(d, a) for a, d in zip(q[:3], (1, 2, 0))]
    far = corner(after(q[3], *two))
    line = all_sum(after(line, *two))
    one = [swap(d, q_near[d + 1] + two[d]) for d in (2, 1, 0)]
    mine, theirs = small(total_kernel, (core,), (after(q_near[0], line), far, *one), ROWS, "total")
    theirs = other_core(theirs)
    d_image, d_text = small(grad_kernel, (par, core), (image_embed, text_embed, mine, theirs), ROWS, "grad")
    return d_image, d_text, line[:3] / total


def solution(mesh):
    fine = Mesh(mesh.devices.reshape(SIZES), AXES)
    wide = P(AXES, None)
    return jax.shard_map(
        body, mesh=fine, in_specs=(wide, wide, P(), P()), out_specs=(wide, wide, P()), check_vma=False
    )
```

```python
import functools

import jax
import jax.numpy as jnp
import numpy as np
from jax import lax
from jax.experimental import pallas as pl
from jax.experimental.pallas import tpu as pltpu
from jax.sharding import Mesh, PartitionSpec as P

EPS = 1e-06
AXES = ("zh", "c", "y", "x", "zl")
SIZES = (2, 2, 4, 4, 2)
ROWS = 128
UNIT = 256
E = 768
CHUNKS = 8
NEAR = 4
CUTS = ((0, 88), (88, 176), (176, 256))
HALF = NEAR * ROWS
SUB = 256
MIB = 1024 * 1024
F32 = jnp.float32
BF16 = jnp.bfloat16


def pairs(move):
    out = []
    for here in range(128):
        zh, c, y, x, zl = (int(v) for v in np.unravel_index(here, SIZES))
        c, x, y, z = move(c, x, y, 2 * zh + zl)
        there = np.ravel_multi_index((z // 2, c, y, x, z % 2), SIZES)
        out.append((here, int(there)))
    return out


def image_mate(v):
    return v ^ 1


def text_mate(v):
    return (((v + 1) ^ 1) - 1) % 4


def across(dim):
    def move(c, x, y, z):
        at = [x, y, z]
        at[dim] = (image_mate if c == 0 else text_mate)(at[dim])
        return (c, *at)

    return pairs(move)


def other_core(a):
    return lax.ppermute(a, AXES, pairs(lambda c, x, y, z: (1 - c, x, y, z)))


def swap(dim, a):
    return lax.ppermute(a, AXES, across(dim))


def split(x):
    hi = x.astype(BF16)
    return hi, (x - hi.astype(F32)).astype(BF16)


def unit(x):
    return x * lax.rsqrt(jnp.sum(x * x, axis=1, keepdims=True) + EPS)


def mm(a, b, dims):
    return lax.dot_general(a, b, (dims, ((), ())), preferred_element_type=F32)


def mm3(a, b, dims):
    return mm(a[0], b[0], dims) + mm(a[0], b[1], dims) + mm(a[1], b[0], dims)


def fold(x):
    return jnp.sum(x.reshape(-1, 8, x.shape[-1]), axis=0)


def prep_images(c, d_refs, e_refs, hi_ref, lo_ref, first=0):
    for k, (d_ref, e_ref) in enumerate(zip(d_refs, e_refs)):
        hi, lo = split(unit(jnp.where(c == 0, d_ref[:ROWS], e_ref[ROWS:])))
        rows = pl.ds((first + k) * ROWS, ROWS)
        hi_ref[rows] = hi
        lo_ref[rows] = lo


def prep_text(c, d_ref, e_ref, hi_ref, lo_ref, k):
    hi, lo = split(unit(jnp.where(c == 0, e_ref[...], d_ref[...])))
    hi_ref[k] = hi
    lo_ref[k] = lo


def work(par, ts, tasks, same, sums, totals):
    def image(j):
        rows = pl.ds(tasks[j][4], SUB)
        return tasks[j][1][rows], tasks[j][2][rows]

    n = len(tasks)
    totals = list(totals)
    ahead = mm3(image(0), ts[tasks[0][0]], ((1,), (1,)))
    coefs = None
    for j in range(n + 1):
        dots = ahead
        if j + 1 < n:
            ahead = mm3(image(j + 1), ts[tasks[j + 1][0]], ((1,), (1,)))
        if coefs is not None:
            at, _, _, partial, first = tasks[j - 1]
            partial[pl.ds(first, SUB)] += mm3(coefs, ts[at], ((1,), (0,)))
            part = mm3(coefs, image(j - 1), ((0,), (0,)))
            totals[at] = part if totals[at] is None else totals[at] + part
        if j < n:
            logits = par[0] * dots + par[1]
            e = jnp.exp(logits)
            u = 1.0 + e
            r = 1.0 / u
            loss = jnp.log(u) + (e - (u - 1.0)) * r
            coef = e * r
            if same is not None and j == 0:
                coef = jnp.where(same, -r, coef)
                loss = jnp.where(same, loss - logits, loss)
            sums[0] += fold(loss)
            sums[1] += fold(coef * dots)
            sums[2] += fold(coef)
            coefs = split(coef)
    return totals


def total_kernel(core, *refs):
    parts, mine, theirs = refs[:-2], refs[-2], refs[-1]

    def put(a, b):
        for half, dest in ((a, mine), (b, theirs)):
            rows = pl.ds(half * ROWS, ROWS)
            dest[...] = (parts[0][rows] + parts[1][rows]) + (parts[2][rows] + parts[3][rows]) + parts[4][rows]

    @pl.when(core[0] == 0)
    def _():
        put(0, 1)

    @pl.when(core[0] == 1)
    def _():
        put(1, 0)


def grad_of(embed, direction, out):
    scale = lax.rsqrt(jnp.sum(embed * embed, axis=1, keepdims=True) + EPS)
    u = embed * scale
    out[...] = scale * (direction - u * jnp.sum(u * direction, axis=1, keepdims=True))


def grad_kernel(par, core, image, text, mine, theirs, d_image, d_text):
    @pl.when(core[0] == 0)
    def _():
        grad_of(image[...], par[0] * mine[...], d_image)
        grad_of(text[...], par[0] * theirs[...], d_text)

    @pl.when(core[0] == 1)
    def _():
        grad_of(image[...], par[0] * theirs[...], d_image)
        grad_of(text[...], par[0] * mine[...], d_text)


def near_kernel(par, core, *refs):
    d_refs, e_refs = refs[:NEAR], refs[NEAR : 2 * NEAR]
    p_txt, p_img, ih, il, th, tl, sums = refs[2 * NEAR :]
    c = core[0]
    p_img[...] = jnp.zeros_like(p_img)
    sums[...] = jnp.zeros_like(sums)
    prep_images(c, d_refs, e_refs, ih, il)
    for k in range(NEAR):
        prep_text(c, d_refs[k], e_refs[k], th, tl, k)
    row = lax.broadcasted_iota(jnp.int32, (SUB, UNIT), 0)
    col = lax.broadcasted_iota(jnp.int32, (SUB, UNIT), 1)

    @pl.loop(0, NEAR // 2)
    def _(i):
        same = (row + c * ROWS == col) & (row < ROWS) & (i == 0)
        ts = [(th[2 * i + h], tl[2 * i + h]) for h in range(2)]
        tasks = [(h, ih, il, p_img, m * SUB) for h in range(2) for m in range(HALF // SUB)]
        out = work(par, ts, tasks, same, sums, [None, None])
        for h in range(2):
            p_txt[2 * i + h] = out[h]


def prep_kernel(core, *refs):
    n = NEAR - 1
    d_refs, e_refs, (ih, il, th, tl) = refs[:n], refs[n : 2 * n], refs[2 * n :]
    prep_images(core[0], d_refs, e_refs, ih, il)
    for k in range(n):
        prep_text(core[0], d_refs[k], e_refs[k], th, tl, k)


def rest_kernel(par, core, *refs):
    d_last, e_last, *mid = refs[:6]
    p_txt, p_img, ihn, iln, thn, tln, i_sums = refs[6:13]
    outs = refs[13:]
    keep_far, send_far = outs[:NEAR], outs[NEAR : 2 * NEAR]
    keep_own, send_own, keep_three, send_three, line, ihf, ilf, thf, tlf, pin, pif, sums = outs[2 * NEAR :]
    keep_near = [keep_own] + [keep_three.at[k] for k in range(NEAR - 1)]
    send_near = [send_own] + [send_three.at[k] for k in range(NEAR - 1)]
    c = core[0]
    last = NEAR - 1
    pin[...] = p_img[...]
    pif[...] = jnp.zeros_like(pif)
    sums[...] = i_sums[...]
    for src, dest in zip(mid, (ihf, ilf, thf, tlf)):
        dest[: src.shape[0]] = src[...]
    prep_images(c, [d_last], [e_last], ihf, ilf, last)
    prep_text(c, d_last, e_last, thf, tlf, last)

    def put(keep, send, total):
        @pl.when(c == 0)
        def _():
            send[...] = total

        @pl.when(c == 1)
        def _():
            keep[...] = total

    @pl.loop(0, NEAR // 2)
    def _(i):
        ts = [(thn[2 * i + h], tln[2 * i + h]) for h in range(2)]
        tasks = [(h, ihf, ilf, pif, m * SUB) for h in range(2) for m in range(HALF // SUB)]
        out = work(par, ts, tasks, None, sums, [p_txt[2 * i], p_txt[2 * i + 1]])
        for v in range(NEAR // 2):

            @pl.when(i == v)
            def _():
                for h in range(2):
                    put(keep_near[2 * v + h], send_near[2 * v + h], out[h])

    @pl.loop(0, NEAR)
    def _(k):
        tasks = [(0, ihn, iln, pin, m * SUB) for m in range(HALF // SUB)]
        tasks += [(0, ihf, ilf, pif, m * SUB) for m in range(HALF // SUB)]
        total = work(par, [(thf[k], tlf[k])], tasks, None, sums, [None])[0]
        for j in range(NEAR):

            @pl.when(k == j)
            def _():
                put(keep_far[j], send_far[j], total)

    lane = lax.broadcasted_iota(jnp.int32, line.shape, 1)
    values = jnp.zeros(line.shape, F32)
    for j, factor in enumerate((1.0, par[0], 1.0)):
        values = jnp.where(lane == j, jnp.sum(sums[j]) * factor, values)
    line[...] = values
    blank = jnp.zeros((ROWS, E), F32)

    @pl.when(c == 0)
    def _():
        for k in range(NEAR):
            for src, dest in ((pin, keep_near[k]), (pif, keep_far[k])):
                dest[:ROWS] = src[pl.ds(k * ROWS, ROWS)]
                dest[ROWS:] = blank

    @pl.when(c == 1)
    def _():
        for k in range(NEAR):
            for src, dest in ((pin, send_near[k]), (pif, send_far[k])):
                dest[:ROWS] = blank
                dest[ROWS:] = src[pl.ds(k * ROWS, ROWS)]


SMEM = pl.BlockSpec(memory_space=pltpu.SMEM)
VMEM = pl.BlockSpec(memory_space=pltpu.VMEM)
SUMS = jax.ShapeDtypeStruct((3, 8, UNIT), F32)
CHUNK = jax.ShapeDtypeStruct((UNIT, E), F32)
THREE = jax.ShapeDtypeStruct((NEAR - 1, UNIT, E), F32)
FOUR = jax.ShapeDtypeStruct((NEAR, UNIT, E), F32)


def cost(pairs_done):
    return pl.CostEstimate(flops=0 * pairs_done, bytes_accessed=4 * UNIT * E, transcendentals=0)


def near_block(par, core, ds, es):
    image = jax.ShapeDtypeStruct((HALF, E), BF16)
    text = jax.ShapeDtypeStruct((NEAR, UNIT, E), BF16)
    return pl.pallas_call(
        near_kernel,
        out_shape=(FOUR, jax.ShapeDtypeStruct((HALF, E), F32), image, image, text, text, SUMS),
        in_specs=[SMEM, SMEM] + [VMEM] * (2 * NEAR),
        out_specs=(VMEM,) * 7,
        compiler_params=pltpu.CompilerParams(vmem_limit_bytes=16 * MIB),
        cost_estimate=cost(NEAR * NEAR * ROWS * UNIT),
        name="near_block",
    )(par, core, *ds, *es)


def prep_block(core, ds, es):
    n = NEAR - 1
    image = jax.ShapeDtypeStruct((n * ROWS, E), BF16)
    text = jax.ShapeDtypeStruct((n, UNIT, E), BF16)
    return pl.pallas_call(
        prep_kernel,
        out_shape=(image, image, text, text),
        in_specs=[SMEM] + [VMEM] * (2 * n),
        out_specs=(VMEM,) * 4,
        compiler_params=pltpu.CompilerParams(vmem_limit_bytes=16 * MIB),
        cost_estimate=cost(0),
        name="prep_block",
    )(core, *ds, *es)


def rest_block(par, core, arrays):
    image = pltpu.VMEM((HALF, E), BF16)
    text = pltpu.VMEM((NEAR, UNIT, E), BF16)
    return pl.pallas_call(
        rest_kernel,
        out_shape=(CHUNK,) * (2 * NEAR + 2) + (THREE, THREE, jax.ShapeDtypeStruct((128, 128), F32)),
        in_specs=[SMEM, SMEM] + [VMEM] * len(arrays),
        out_specs=(VMEM,) * (2 * NEAR + 5),
        scratch_shapes=[image, image, text, text, pltpu.VMEM((HALF, E), F32), pltpu.VMEM((HALF, E), F32), pltpu.VMEM((3, 8, UNIT), F32)],
        compiler_params=pltpu.CompilerParams(vmem_limit_bytes=24 * MIB),
        cost_estimate=cost((CHUNKS * CHUNKS - NEAR * NEAR) * ROWS * UNIT),
        name="rest_block",
    )(par, core, *arrays)


def small(kernel, scalars, arrays, rows, name, outs=2):
    return pl.pallas_call(
        kernel,
        out_shape=(jax.ShapeDtypeStruct((rows, E), F32),) * outs,
        in_specs=[SMEM] * len(scalars) + [VMEM] * len(arrays),
        out_specs=(VMEM,) * outs,
        compiler_params=pltpu.CompilerParams(vmem_limit_bytes=8 * MIB),
        cost_estimate=cost(0),
        name=name,
    )(*scalars, *arrays)


def corner(a):
    def move(c, x, y, z):
        mate = image_mate if c == 0 else text_mate
        return (c, mate(x), mate(y), mate(z))

    return lax.ppermute(a, AXES, pairs(move))


def after(a, *others):
    return lax.optimization_barrier((a, *others))[0]


def exchange(line, axes):
    return jnp.sum(lax.all_to_all(line, axes, 0, 0, tiled=True), axis=0, keepdims=True)


def body(image_embed, text_embed, log_temp, bias):
    c = lax.axis_index("c")
    total = image_embed.shape[0] * 128
    temp = jnp.exp(log_temp)
    par = jnp.concatenate([temp, bias])
    core = c.astype(jnp.int32).reshape(1)
    img_rec, txt_rec = other_core(image_embed), other_core(text_embed)
    first = c == 0
    own = jnp.concatenate([jnp.where(first, image_embed, txt_rec), jnp.where(first, img_rec, text_embed)])
    e_own = jnp.concatenate([jnp.where(first, text_embed, img_rec), jnp.where(first, txt_rec, image_embed)])
    one = [swap(d, own) for d in range(3)]
    zx = swap(0, one[2])
    yz = swap(2, one[1])
    xy = swap(1, one[0])
    near, e_near = [own] + one, [e_own] + [other_core(after(a, *one)) for a in one]
    before = near_block(par, core, near, e_near)
    two = [after(a, before[-1]) for a in (xy, yz, zx)]
    last = jnp.concatenate([swap(d, a[lo:hi]) for d, a, (lo, hi) in zip((2, 0, 1), two, CUTS)])
    rest = [*two, last]
    e_rest = [other_core(after(a, *two)) for a in two] + [other_core(last)]
    mid = prep_block(core, rest[:3], e_rest[:3])
    outs = rest_block(par, core, [rest[3], e_rest[3], *mid, *before])
    keep, send, (keep_own, send_own, keep_near, send_near, line) = outs[:NEAR], outs[NEAR : 2 * NEAR], outs[2 * NEAR :]
    q_own = keep_own + other_core(send_own)
    q = [k + other_core(s) for k, s in zip(keep, send)]
    got = other_core(after(send_near, *q[:3]))
    q_near = [keep_near[k] + got[k] for k in range(NEAR - 1)]
    two = [swap(d, a) for a, d in zip(q[:3], (1, 2, 0))]
    far = corner(after(q[3], *two))
    line = exchange(after(line, *two), AXES)
    core_b, line = lax.optimization_barrier((core, line))
    one = [swap(d, q_near[d] + two[d]) for d in (2, 1, 0)]
    mine, theirs = small(total_kernel, (core_b,), (q_own, far, *one), ROWS, "total")
    theirs = other_core(theirs)
    d_image, d_text = small(grad_kernel, (par, core), (image_embed, text_embed, mine, theirs), ROWS, "grad")
    return d_image, d_text, line[0, :3] / total


def solution(mesh):
    fine = Mesh(mesh.devices.reshape(SIZES), AXES)
    wide = P(AXES, None)
    return jax.shard_map(
        body, mesh=fine, in_specs=(wide, wide, P(), P()), out_specs=(wide, wide, P()), check_vma=False
    )
```

```python
import functools

import jax
import jax.numpy as jnp
import numpy as np
from jax import lax
from jax.experimental import pallas as pl
from jax.experimental.pallas import tpu as pltpu
from jax.sharding import Mesh, PartitionSpec as P

EPS = 1e-06
AXES = ("zh", "c", "y", "x", "zl")
SIZES = (2, 2, 4, 4, 2)
ROWS = 128
UNIT = 256
E = 768
CHUNKS = 8
NEAR = 4
CUTS = ((0, 88), (88, 176), (176, 256))
HALF = NEAR * ROWS
SUB = 256
PAIR = 2 * UNIT
MIB = 1024 * 1024
F32 = jnp.float32
BF16 = jnp.bfloat16


def pairs(move):
    out = []
    for here in range(128):
        zh, c, y, x, zl = (int(v) for v in np.unravel_index(here, SIZES))
        c, x, y, z = move(c, x, y, 2 * zh + zl)
        there = np.ravel_multi_index((z // 2, c, y, x, z % 2), SIZES)
        out.append((here, int(there)))
    return out


def image_mate(v):
    return v ^ 1


def text_mate(v):
    return (((v + 1) ^ 1) - 1) % 4


def across(dim):
    def move(c, x, y, z):
        at = [x, y, z]
        at[dim] = (image_mate if c == 0 else text_mate)(at[dim])
        return (c, *at)

    return pairs(move)


def other_core(a):
    return lax.ppermute(a, AXES, pairs(lambda c, x, y, z: (1 - c, x, y, z)))


def swap(dim, a):
    return lax.ppermute(a, AXES, across(dim))


def split(x):
    hi = x.astype(BF16)
    return hi, (x - hi.astype(F32)).astype(BF16)


def unit(x):
    return x * lax.rsqrt(jnp.sum(x * x, axis=1, keepdims=True) + EPS)


def mm(a, b, dims):
    return lax.dot_general(a, b, (dims, ((), ())), preferred_element_type=F32)


def mm3(a, b, dims):
    return mm(a[0], b[0], dims) + mm(a[0], b[1], dims) + mm(a[1], b[0], dims)


def fold(x):
    return jnp.sum(x.reshape(-1, 8, x.shape[-1]), axis=0)


def prep_images(c, d_refs, e_refs, hi_ref, lo_ref, first=0):
    for k, (d_ref, e_ref) in enumerate(zip(d_refs, e_refs)):
        hi, lo = split(unit(jnp.where(c == 0, d_ref[:ROWS], e_ref[ROWS:])))
        rows = pl.ds((first + k) * ROWS, ROWS)
        hi_ref[rows] = hi
        lo_ref[rows] = lo


def prep_text(c, d_ref, e_ref, hi_ref, lo_ref, k):
    hi, lo = split(unit(jnp.where(c == 0, e_ref[...], d_ref[...])))
    hi_ref[k] = hi
    lo_ref[k] = lo


def work(par, text, tasks, same, sums, totals):
    def image(j):
        rows = pl.ds(tasks[j][4], SUB)
        return tasks[j][1][rows], tasks[j][2][rows]

    n = len(tasks)
    totals = list(totals)
    ahead = mm3(image(0), text(tasks[0][0]), ((1,), (1,)))
    coefs = None
    for j in range(n + 1):
        dots = ahead
        if j + 1 < n:
            ahead = mm3(image(j + 1), text(tasks[j + 1][0]), ((1,), (1,)))
        if coefs is not None:
            at, _, _, partial, first = tasks[j - 1]
            partial[pl.ds(first, SUB)] += mm3(coefs, text(at), ((1,), (0,)))
            part = mm3(coefs, image(j - 1), ((0,), (0,)))
            totals[at] = part if totals[at] is None else totals[at] + part
        if j < n:
            logits = par[0] * dots + par[1]
            e = jnp.exp(logits)
            u = 1.0 + e
            r = 1.0 / u
            loss = jnp.log(u) + (e - (u - 1.0)) * r
            coef = e * r
            if same is not None and j == 0:
                coef = jnp.where(same, -r, coef)
                loss = jnp.where(same, loss - logits, loss)
            sums[0] += fold(loss)
            sums[1] += fold(coef * dots)
            sums[2] += fold(coef)
            coefs = split(coef)
    return totals


def total_kernel(core, *refs):
    parts, mine, theirs = refs[:-2], refs[-2], refs[-1]

    def put(a, b):
        for half, dest in ((a, mine), (b, theirs)):
            rows = pl.ds(half * ROWS, ROWS)
            dest[...] = (parts[0][rows] + parts[1][rows]) + (parts[2][rows] + parts[3][rows]) + parts[4][rows]

    @pl.when(core[0] == 0)
    def _():
        put(0, 1)

    @pl.when(core[0] == 1)
    def _():
        put(1, 0)


def grad_of(embed, direction, out):
    scale = lax.rsqrt(jnp.sum(embed * embed, axis=1, keepdims=True) + EPS)
    u = embed * scale
    out[...] = scale * (direction - u * jnp.sum(u * direction, axis=1, keepdims=True))


def grad_kernel(par, core, image, text, mine, theirs, d_image, d_text):
    @pl.when(core[0] == 0)
    def _():
        grad_of(image[...], par[0] * mine[...], d_image)
        grad_of(text[...], par[0] * theirs[...], d_text)

    @pl.when(core[0] == 1)
    def _():
        grad_of(image[...], par[0] * theirs[...], d_image)
        grad_of(text[...], par[0] * mine[...], d_text)


def two_of(hi, lo, k):
    return hi[pl.ds(k, 2)].reshape(PAIR, E), lo[pl.ds(k, 2)].reshape(PAIR, E)


def near_kernel(par, core, *refs):
    d_refs, e_refs = refs[:NEAR], refs[NEAR : 2 * NEAR]
    p_txt, p_img, ih, il, th, tl, sums = refs[2 * NEAR :]
    c = core[0]
    p_img[...] = jnp.zeros_like(p_img)
    sums[...] = jnp.zeros_like(sums)
    prep_images(c, d_refs, e_refs, ih, il)
    for k in range(NEAR):
        prep_text(c, d_refs[k], e_refs[k], th, tl, k)
    row = lax.broadcasted_iota(jnp.int32, (SUB, PAIR), 0)
    col = lax.broadcasted_iota(jnp.int32, (SUB, PAIR), 1)

    same = (row + c * ROWS == col) & (row < ROWS)
    tasks = [(h, ih, il, p_img, m * SUB) for h in range(2) for m in range(HALF // SUB)]
    out = work(par, lambda h: two_of(th, tl, 2 * h), tasks, same, sums, [None, None])
    for h in range(2):
        p_txt[2 * h : 2 * h + 2] = out[h].reshape(2, UNIT, E)


def prep_kernel(core, *refs):
    n = NEAR - 1
    d_refs, e_refs, (ih, il, th, tl) = refs[:n], refs[n : 2 * n], refs[2 * n :]
    prep_images(core[0], d_refs, e_refs, ih, il)
    for k in range(n):
        prep_text(core[0], d_refs[k], e_refs[k], th, tl, k)


def rest_kernel(par, core, *refs):
    d_last, e_last, *mid = refs[:6]
    p_txt, p_img, ihn, iln, thn, tln, i_sums = refs[6:13]
    outs = refs[13:]
    keep_far, send_far = outs[:NEAR], outs[NEAR : 2 * NEAR]
    keep_own, send_own, keep_three, send_three, line, ihf, ilf, thf, tlf, pin, pif, sums = outs[2 * NEAR :]
    keep_near = [keep_own] + [keep_three.at[k] for k in range(NEAR - 1)]
    send_near = [send_own] + [send_three.at[k] for k in range(NEAR - 1)]
    c = core[0]
    last = NEAR - 1
    pin[...] = p_img[...]
    pif[...] = jnp.zeros_like(pif)
    sums[...] = i_sums[...]
    for src, dest in zip(mid, (ihf, ilf, thf, tlf)):
        dest[: src.shape[0]] = src[...]
    prep_images(c, [d_last], [e_last], ihf, ilf, last)
    prep_text(c, d_last, e_last, thf, tlf, last)

    def put(keep, send, total):
        @pl.when(c == 0)
        def _():
            send[...] = total

        @pl.when(c == 1)
        def _():
            keep[...] = total

    tasks = [(h, ihf, ilf, pif, m * SUB) for h in range(2) for m in range(HALF // SUB)]
    starts = [p_txt[2 * h : 2 * h + 2].reshape(PAIR, E) for h in range(2)]
    out = work(par, lambda h: two_of(thn, tln, 2 * h), tasks, None, sums, starts)
    for k in range(NEAR):
        put(keep_near[k], send_near[k], out[k // 2][(k % 2) * UNIT : (k % 2 + 1) * UNIT])

    @pl.loop(0, NEAR // 2)
    def _(i):
        tasks = [(0, ihn, iln, pin, m * SUB) for m in range(HALF // SUB)]
        tasks += [(0, ihf, ilf, pif, m * SUB) for m in range(HALF // SUB)]
        total = work(par, lambda h: two_of(thf, tlf, 2 * i), tasks, None, sums, [None])[0]
        for v in range(NEAR // 2):

            @pl.when(i == v)
            def _():
                for h in range(2):
                    put(keep_far[2 * v + h], send_far[2 * v + h], total[h * UNIT : (h + 1) * UNIT])

    lane = lax.broadcasted_iota(jnp.int32, line.shape, 1)
    values = jnp.zeros(line.shape, F32)
    for j, factor in enumerate((1.0, par[0], 1.0)):
        values = jnp.where(lane == j, jnp.sum(sums[j]) * factor, values)
    line[...] = values
    blank = jnp.zeros((ROWS, E), F32)

    @pl.when(c == 0)
    def _():
        for k in range(NEAR):
            for src, dest in ((pin, keep_near[k]), (pif, keep_far[k])):
                dest[:ROWS] = src[pl.ds(k * ROWS, ROWS)]
                dest[ROWS:] = blank

    @pl.when(c == 1)
    def _():
        for k in range(NEAR):
            for src, dest in ((pin, send_near[k]), (pif, send_far[k])):
                dest[:ROWS] = blank
                dest[ROWS:] = src[pl.ds(k * ROWS, ROWS)]


SMEM = pl.BlockSpec(memory_space=pltpu.SMEM)
VMEM = pl.BlockSpec(memory_space=pltpu.VMEM)
SUMS = jax.ShapeDtypeStruct((3, 8, PAIR), F32)
CHUNK = jax.ShapeDtypeStruct((UNIT, E), F32)
THREE = jax.ShapeDtypeStruct((NEAR - 1, UNIT, E), F32)
FOUR = jax.ShapeDtypeStruct((NEAR, UNIT, E), F32)


def cost(pairs_done):
    return pl.CostEstimate(flops=0 * pairs_done, bytes_accessed=4 * UNIT * E, transcendentals=0)


def near_block(par, core, ds, es):
    image = jax.ShapeDtypeStruct((HALF, E), BF16)
    text = jax.ShapeDtypeStruct((NEAR, UNIT, E), BF16)
    return pl.pallas_call(
        near_kernel,
        out_shape=(FOUR, jax.ShapeDtypeStruct((HALF, E), F32), image, image, text, text, SUMS),
        in_specs=[SMEM, SMEM] + [VMEM] * (2 * NEAR),
        out_specs=(VMEM,) * 7,
        compiler_params=pltpu.CompilerParams(vmem_limit_bytes=16 * MIB),
        cost_estimate=cost(NEAR * NEAR * ROWS * UNIT),
        name="near_block",
    )(par, core, *ds, *es)


def prep_block(core, ds, es):
    n = NEAR - 1
    image = jax.ShapeDtypeStruct((n * ROWS, E), BF16)
    text = jax.ShapeDtypeStruct((n, UNIT, E), BF16)
    return pl.pallas_call(
        prep_kernel,
        out_shape=(image, image, text, text),
        in_specs=[SMEM] + [VMEM] * (2 * n),
        out_specs=(VMEM,) * 4,
        compiler_params=pltpu.CompilerParams(vmem_limit_bytes=16 * MIB),
        cost_estimate=cost(0),
        name="prep_block",
    )(core, *ds, *es)


def rest_block(par, core, arrays):
    image = pltpu.VMEM((HALF, E), BF16)
    text = pltpu.VMEM((NEAR, UNIT, E), BF16)
    return pl.pallas_call(
        rest_kernel,
        out_shape=(CHUNK,) * (2 * NEAR + 2) + (THREE, THREE, jax.ShapeDtypeStruct((128, 128), F32)),
        in_specs=[SMEM, SMEM] + [VMEM] * len(arrays),
        out_specs=(VMEM,) * (2 * NEAR + 5),
        scratch_shapes=[image, image, text, text, pltpu.VMEM((HALF, E), F32), pltpu.VMEM((HALF, E), F32), pltpu.VMEM((3, 8, PAIR), F32)],
        compiler_params=pltpu.CompilerParams(vmem_limit_bytes=24 * MIB),
        cost_estimate=cost((CHUNKS * CHUNKS - NEAR * NEAR) * ROWS * UNIT),
        name="rest_block",
    )(par, core, *arrays)


def small(kernel, scalars, arrays, rows, name, outs=2):
    return pl.pallas_call(
        kernel,
        out_shape=(jax.ShapeDtypeStruct((rows, E), F32),) * outs,
        in_specs=[SMEM] * len(scalars) + [VMEM] * len(arrays),
        out_specs=(VMEM,) * outs,
        compiler_params=pltpu.CompilerParams(vmem_limit_bytes=8 * MIB),
        cost_estimate=cost(0),
        name=name,
    )(*scalars, *arrays)


def corner(a):
    def move(c, x, y, z):
        mate = image_mate if c == 0 else text_mate
        return (c, mate(x), mate(y), mate(z))

    return lax.ppermute(a, AXES, pairs(move))


def after(a, *others):
    return lax.optimization_barrier((a, *others))[0]


def exchange(line, axes):
    return jnp.sum(lax.all_to_all(line, axes, 0, 0, tiled=True), axis=0, keepdims=True)


def body(image_embed, text_embed, log_temp, bias):
    c = lax.axis_index("c")
    total = image_embed.shape[0] * 128
    temp = jnp.exp(log_temp)
    par = jnp.concatenate([temp, bias])
    core = c.astype(jnp.int32).reshape(1)
    img_rec, txt_rec = other_core(image_embed), other_core(text_embed)
    first = c == 0
    own = jnp.concatenate([jnp.where(first, image_embed, txt_rec), jnp.where(first, img_rec, text_embed)])
    e_own = jnp.concatenate([jnp.where(first, text_embed, img_rec), jnp.where(first, txt_rec, image_embed)])
    one = [swap(d, own) for d in range(3)]
    zx = swap(0, one[2])
    yz = swap(2, one[1])
    xy = swap(1, one[0])
    near, e_near = [own] + one, [e_own] + [other_core(after(a, *one)) for a in one]
    before = near_block(par, core, near, e_near)
    two = [after(a, before[-1]) for a in (xy, yz, zx)]
    last = jnp.concatenate([swap(d, a[lo:hi]) for d, a, (lo, hi) in zip((2, 0, 1), two, CUTS)])
    rest = [*two, last]
    e_rest = [other_core(after(a, *two)) for a in two] + [other_core(last)]
    mid = prep_block(core, rest[:3], e_rest[:3])
    outs = rest_block(par, core, [rest[3], e_rest[3], *mid, *before])
    keep, send, (keep_own, send_own, keep_near, send_near, line) = outs[:NEAR], outs[NEAR : 2 * NEAR], outs[2 * NEAR :]
    q_own = keep_own + other_core(send_own)
    q = [k + other_core(s) for k, s in zip(keep, send)]
    got = other_core(after(send_near, *q[:3]))
    q_near = [keep_near[k] + got[k] for k in range(NEAR - 1)]
    two = [swap(d, a) for a, d in zip(q[:3], (1, 2, 0))]
    far = corner(after(q[3], *two))
    line = exchange(after(line, *two), AXES)
    core_b, line = lax.optimization_barrier((core, line))
    one = [swap(d, q_near[d] + two[d]) for d in (2, 1, 0)]
    mine, theirs = small(total_kernel, (core_b,), (q_own, far, *one), ROWS, "total")
    theirs = other_core(theirs)
    d_image, d_text = small(grad_kernel, (par, core), (image_embed, text_embed, mine, theirs), ROWS, "grad")
    return d_image, d_text, line[0, :3] / total


def solution(mesh):
    fine = Mesh(mesh.devices.reshape(SIZES), AXES)
    wide = P(AXES, None)
    return jax.shard_map(
        body, mesh=fine, in_specs=(wide, wide, P(), P()), out_specs=(wide, wide, P()), check_vma=False
    )
```

```python
import functools

import jax
import jax.numpy as jnp
import numpy as np
from jax import lax
from jax.experimental import pallas as pl
from jax.experimental.pallas import tpu as pltpu
from jax.sharding import Mesh, PartitionSpec as P

EPS = 1e-06
AXES = ("zh", "c", "y", "x", "zl")
SIZES = (2, 2, 4, 4, 2)
ROWS = 128
UNIT = 256
E = 768
CHUNKS = 8
NEAR = 4
CUTS = ((0, 88), (88, 176), (176, 256))
HALF = NEAR * ROWS
SUB = 256
PAIR = 2 * UNIT
MIB = 1024 * 1024
F32 = jnp.float32
BF16 = jnp.bfloat16


def pairs(move):
    out = []
    for here in range(128):
        zh, c, y, x, zl = (int(v) for v in np.unravel_index(here, SIZES))
        c, x, y, z = move(c, x, y, 2 * zh + zl)
        there = np.ravel_multi_index((z // 2, c, y, x, z % 2), SIZES)
        out.append((here, int(there)))
    return out


def image_mate(v):
    return v ^ 1


def text_mate(v):
    return (((v + 1) ^ 1) - 1) % 4


def across(dim):
    def move(c, x, y, z):
        at = [x, y, z]
        at[dim] = (image_mate if c == 0 else text_mate)(at[dim])
        return (c, *at)

    return pairs(move)


def other_core(a):
    return lax.ppermute(a, AXES, pairs(lambda c, x, y, z: (1 - c, x, y, z)))


def swap(dim, a):
    return lax.ppermute(a, AXES, across(dim))


def split(x):
    hi = x.astype(BF16)
    return hi, (x - hi.astype(F32)).astype(BF16)


def unit(x):
    return x * lax.rsqrt(jnp.sum(x * x, axis=1, keepdims=True) + EPS)


def mm(a, b, dims):
    return lax.dot_general(a, b, (dims, ((), ())), preferred_element_type=F32)


def mm3(a, b, dims):
    return mm(a[0], b[0], dims) + mm(a[0], b[1], dims) + mm(a[1], b[0], dims)


def fold(x):
    return jnp.sum(x.reshape(-1, 8, x.shape[-1]), axis=0)


def prep_images(c, d_refs, e_refs, hi_ref, lo_ref, first=0):
    for k, (d_ref, e_ref) in enumerate(zip(d_refs, e_refs)):
        hi, lo = split(unit(jnp.where(c == 0, d_ref[:ROWS], e_ref[ROWS:])))
        rows = pl.ds((first + k) * ROWS, ROWS)
        hi_ref[rows] = hi
        lo_ref[rows] = lo


def prep_text(c, d_ref, e_ref, hi_ref, lo_ref, k):
    hi, lo = split(unit(jnp.where(c == 0, e_ref[...], d_ref[...])))
    hi_ref[k] = hi
    lo_ref[k] = lo


def work(par, text, tasks, same, sums, totals):
    def image(j):
        rows = pl.ds(tasks[j][4], SUB)
        return tasks[j][1][rows], tasks[j][2][rows]

    n = len(tasks)
    totals = list(totals)
    ahead = mm3(image(0), text(tasks[0][0]), ((1,), (1,)))
    coefs = None
    for j in range(n + 1):
        dots = ahead
        if j + 1 < n:
            ahead = mm3(image(j + 1), text(tasks[j + 1][0]), ((1,), (1,)))
        if coefs is not None:
            at, _, _, partial, first = tasks[j - 1]
            partial[pl.ds(first, SUB)] += mm3(coefs, text(at), ((1,), (0,)))
            part = mm3(coefs, image(j - 1), ((0,), (0,)))
            totals[at] = part if totals[at] is None else totals[at] + part
        if j < n:
            logits = par[0] * dots + par[1]
            e = jnp.exp(logits)
            u = 1.0 + e
            r = 1.0 / u
            loss = jnp.log(u) + (e - (u - 1.0)) * r
            coef = e * r
            if same is not None and j == 0:
                coef = jnp.where(same, -r, coef)
                loss = jnp.where(same, loss - logits, loss)
            sums[0] += fold(loss)
            sums[1] += fold(coef * dots)
            sums[2] += fold(coef)
            coefs = split(coef)
    return totals


def total_kernel(core, *refs):
    parts, mine, theirs = refs[:-2], refs[-2], refs[-1]

    def put(a, b):
        for half, dest in ((a, mine), (b, theirs)):
            rows = pl.ds(half * ROWS, ROWS)
            dest[...] = (parts[0][rows] + parts[1][rows]) + (parts[2][rows] + parts[3][rows]) + parts[4][rows]

    @pl.when(core[0] == 0)
    def _():
        put(0, 1)

    @pl.when(core[0] == 1)
    def _():
        put(1, 0)


def grad_of(embed, direction, out):
    scale = lax.rsqrt(jnp.sum(embed * embed, axis=1, keepdims=True) + EPS)
    u = embed * scale
    out[...] = scale * (direction - u * jnp.sum(u * direction, axis=1, keepdims=True))


def grad_kernel(par, core, image, text, mine, theirs, d_image, d_text):
    @pl.when(core[0] == 0)
    def _():
        grad_of(image[...], par[0] * mine[...], d_image)
        grad_of(text[...], par[0] * theirs[...], d_text)

    @pl.when(core[0] == 1)
    def _():
        grad_of(image[...], par[0] * theirs[...], d_image)
        grad_of(text[...], par[0] * mine[...], d_text)


def two_of(hi, lo, k):
    return hi[pl.ds(k, 2)].reshape(PAIR, E), lo[pl.ds(k, 2)].reshape(PAIR, E)


def near_kernel(par, core, *refs):
    d_refs, e_refs = refs[:NEAR], refs[NEAR : 2 * NEAR]
    p_txt, p_img, ih, il, th, tl, sums = refs[2 * NEAR :]
    c = core[0]
    p_img[...] = jnp.zeros_like(p_img)
    sums[...] = jnp.zeros_like(sums)
    prep_images(c, d_refs, e_refs, ih, il)
    for k in range(NEAR):
        prep_text(c, d_refs[k], e_refs[k], th, tl, k)
    row = lax.broadcasted_iota(jnp.int32, (SUB, PAIR), 0)
    col = lax.broadcasted_iota(jnp.int32, (SUB, PAIR), 1)

    @pl.loop(0, NEAR // 2)
    def _(i):
        same = (row + c * ROWS == col) & (row < ROWS) & (i == 0)
        tasks = [(0, ih, il, p_img, m * SUB) for m in range(HALF // SUB)]
        out = work(par, lambda h: two_of(th, tl, 2 * i), tasks, same, sums, [None])[0]
        p_txt[pl.ds(2 * i, 2)] = out.reshape(2, UNIT, E)


def prep_kernel(core, *refs):
    n = NEAR - 1
    d_refs, e_refs, (ih, il, th, tl) = refs[:n], refs[n : 2 * n], refs[2 * n :]
    prep_images(core[0], d_refs, e_refs, ih, il)
    for k in range(n):
        prep_text(core[0], d_refs[k], e_refs[k], th, tl, k)


def rest_kernel(par, core, *refs):
    d_last, e_last, *mid = refs[:6]
    p_txt, p_img, ihn, iln, thn, tln, i_sums = refs[6:13]
    outs = refs[13:]
    keep_far, send_far = outs[:NEAR], outs[NEAR : 2 * NEAR]
    keep_own, send_own, keep_three, send_three, line, ihf, ilf, thf, tlf, pin, pif, sums = outs[2 * NEAR :]
    keep_near = [keep_own] + [keep_three.at[k] for k in range(NEAR - 1)]
    send_near = [send_own] + [send_three.at[k] for k in range(NEAR - 1)]
    c = core[0]
    last = NEAR - 1
    pin[...] = p_img[...]
    pif[...] = jnp.zeros_like(pif)
    sums[...] = i_sums[...]
    for src, dest in zip(mid, (ihf, ilf, thf, tlf)):
        dest[: src.shape[0]] = src[...]
    prep_images(c, [d_last], [e_last], ihf, ilf, last)
    prep_text(c, d_last, e_last, thf, tlf, last)

    def put(keep, send, total):
        @pl.when(c == 0)
        def _():
            send[...] = total

        @pl.when(c == 1)
        def _():
            keep[...] = total

    tasks = [(h, ihf, ilf, pif, m * SUB) for h in range(2) for m in range(HALF // SUB)]
    starts = [p_txt[2 * h : 2 * h + 2].reshape(PAIR, E) for h in range(2)]
    out = work(par, lambda h: two_of(thn, tln, 2 * h), tasks, None, sums, starts)
    for k in range(NEAR):
        put(keep_near[k], send_near[k], out[k // 2][(k % 2) * UNIT : (k % 2 + 1) * UNIT])

    @pl.loop(0, NEAR // 2)
    def _(i):
        tasks = [(0, ihn, iln, pin, m * SUB) for m in range(HALF // SUB)]
        tasks += [(0, ihf, ilf, pif, m * SUB) for m in range(HALF // SUB)]
        total = work(par, lambda h: two_of(thf, tlf, 2 * i), tasks, None, sums, [None])[0]
        for v in range(NEAR // 2):

            @pl.when(i == v)
            def _():
                for h in range(2):
                    put(keep_far[2 * v + h], send_far[2 * v + h], total[h * UNIT : (h + 1) * UNIT])

    lane = lax.broadcasted_iota(jnp.int32, line.shape, 1)
    values = jnp.zeros(line.shape, F32)
    for j, factor in enumerate((1.0, par[0], 1.0)):
        values = jnp.where(lane == j, jnp.sum(sums[j]) * factor, values)
    line[...] = values
    blank = jnp.zeros((ROWS, E), F32)

    @pl.when(c == 0)
    def _():
        for k in range(NEAR):
            for src, dest in ((pin, keep_near[k]), (pif, keep_far[k])):
                dest[:ROWS] = src[pl.ds(k * ROWS, ROWS)]
                dest[ROWS:] = blank

    @pl.when(c == 1)
    def _():
        for k in range(NEAR):
            for src, dest in ((pin, send_near[k]), (pif, send_far[k])):
                dest[:ROWS] = blank
                dest[ROWS:] = src[pl.ds(k * ROWS, ROWS)]


SMEM = pl.BlockSpec(memory_space=pltpu.SMEM)
VMEM = pl.BlockSpec(memory_space=pltpu.VMEM)
SUMS = jax.ShapeDtypeStruct((3, 8, PAIR), F32)
CHUNK = jax.ShapeDtypeStruct((UNIT, E), F32)
THREE = jax.ShapeDtypeStruct((NEAR - 1, UNIT, E), F32)
FOUR = jax.ShapeDtypeStruct((NEAR, UNIT, E), F32)


def cost(pairs_done):
    return pl.CostEstimate(flops=0 * pairs_done, bytes_accessed=4 * UNIT * E, transcendentals=0)


def near_block(par, core, ds, es):
    image = jax.ShapeDtypeStruct((HALF, E), BF16)
    text = jax.ShapeDtypeStruct((NEAR, UNIT, E), BF16)
    return pl.pallas_call(
        near_kernel,
        out_shape=(FOUR, jax.ShapeDtypeStruct((HALF, E), F32), image, image, text, text, SUMS),
        in_specs=[SMEM, SMEM] + [VMEM] * (2 * NEAR),
        out_specs=(VMEM,) * 7,
        compiler_params=pltpu.CompilerParams(vmem_limit_bytes=16 * MIB),
        cost_estimate=cost(NEAR * NEAR * ROWS * UNIT),
        name="near_block",
    )(par, core, *ds, *es)


def prep_block(core, ds, es):
    n = NEAR - 1
    image = jax.ShapeDtypeStruct((n * ROWS, E), BF16)
    text = jax.ShapeDtypeStruct((n, UNIT, E), BF16)
    return pl.pallas_call(
        prep_kernel,
        out_shape=(image, image, text, text),
        in_specs=[SMEM] + [VMEM] * (2 * n),
        out_specs=(VMEM,) * 4,
        compiler_params=pltpu.CompilerParams(vmem_limit_bytes=16 * MIB),
        cost_estimate=cost(0),
        name="prep_block",
    )(core, *ds, *es)


def rest_block(par, core, arrays):
    image = pltpu.VMEM((HALF, E), BF16)
    text = pltpu.VMEM((NEAR, UNIT, E), BF16)
    return pl.pallas_call(
        rest_kernel,
        out_shape=(CHUNK,) * (2 * NEAR + 2) + (THREE, THREE, jax.ShapeDtypeStruct((128, 128), F32)),
        in_specs=[SMEM, SMEM] + [VMEM] * len(arrays),
        out_specs=(VMEM,) * (2 * NEAR + 5),
        scratch_shapes=[image, image, text, text, pltpu.VMEM((HALF, E), F32), pltpu.VMEM((HALF, E), F32), pltpu.VMEM((3, 8, PAIR), F32)],
        compiler_params=pltpu.CompilerParams(vmem_limit_bytes=24 * MIB),
        cost_estimate=cost((CHUNKS * CHUNKS - NEAR * NEAR) * ROWS * UNIT),
        name="rest_block",
    )(par, core, *arrays)


def small(kernel, scalars, arrays, rows, name, outs=2):
    return pl.pallas_call(
        kernel,
        out_shape=(jax.ShapeDtypeStruct((rows, E), F32),) * outs,
        in_specs=[SMEM] * len(scalars) + [VMEM] * len(arrays),
        out_specs=(VMEM,) * outs,
        compiler_params=pltpu.CompilerParams(vmem_limit_bytes=8 * MIB),
        cost_estimate=cost(0),
        name=name,
    )(*scalars, *arrays)


def corner(a):
    def move(c, x, y, z):
        mate = image_mate if c == 0 else text_mate
        return (c, mate(x), mate(y), mate(z))

    return lax.ppermute(a, AXES, pairs(move))


def after(a, *others):
    return lax.optimization_barrier((a, *others))[0]


def exchange(line, axes):
    return jnp.sum(lax.all_to_all(line, axes, 0, 0, tiled=True), axis=0, keepdims=True)


def body(image_embed, text_embed, log_temp, bias):
    c = lax.axis_index("c")
    total = image_embed.shape[0] * 128
    temp = jnp.exp(log_temp)
    par = jnp.concatenate([temp, bias])
    core = c.astype(jnp.int32).reshape(1)
    img_rec, txt_rec = other_core(image_embed), other_core(text_embed)
    first = c == 0
    own = jnp.concatenate([jnp.where(first, image_embed, txt_rec), jnp.where(first, img_rec, text_embed)])
    e_own = jnp.concatenate([jnp.where(first, text_embed, img_rec), jnp.where(first, txt_rec, image_embed)])
    one = [swap(d, own) for d in range(3)]
    zx = swap(0, one[2])
    yz = swap(2, one[1])
    xy = swap(1, one[0])
    near, e_near = [own] + one, [e_own] + [other_core(after(a, *one)) for a in one]
    before = near_block(par, core, near, e_near)
    two = [after(a, before[-1]) for a in (xy, yz, zx)]
    last = jnp.concatenate([swap(d, a[lo:hi]) for d, a, (lo, hi) in zip((2, 0, 1), two, CUTS)])
    rest = [*two, last]
    e_rest = [other_core(after(a, *two)) for a in two] + [other_core(last)]
    mid = prep_block(core, rest[:3], e_rest[:3])
    outs = rest_block(par, core, [rest[3], e_rest[3], *mid, *before])
    keep, send, (keep_own, send_own, keep_near, send_near, line) = outs[:NEAR], outs[NEAR : 2 * NEAR], outs[2 * NEAR :]
    q_own = keep_own + other_core(send_own)
    q = [k + other_core(s) for k, s in zip(keep, send)]
    got = other_core(after(send_near, *q[:3]))
    q_near = [keep_near[k] + got[k] for k in range(NEAR - 1)]
    two = [swap(d, a) for a, d in zip(q[:3], (1, 2, 0))]
    far = corner(after(q[3], *two))
    line = exchange(after(line, *two), AXES)
    core_b, line = lax.optimization_barrier((core, line))
    one = [swap(d, q_near[d] + two[d]) for d in (2, 1, 0)]
    mine, theirs = small(total_kernel, (core_b,), (q_own, far, *one), ROWS, "total")
    theirs = other_core(theirs)
    d_image, d_text = small(grad_kernel, (par, core), (image_embed, text_embed, mine, theirs), ROWS, "grad")
    return d_image, d_text, line[0, :3] / total


def solution(mesh):
    fine = Mesh(mesh.devices.reshape(SIZES), AXES)
    wide = P(AXES, None)
    return jax.shard_map(
        body, mesh=fine, in_specs=(wide, wide, P(), P()), out_specs=(wide, wide, P()), check_vma=False
    )
```
